32 devices in a mesh: grp: 2 (over y), lat: 4 (over z), lon: 4 (over x, core).
Axes of the slice: x: 2, y: 2, z: 4, core: 2. Of those that a mesh axis runs over, the one named last changes fastest.
Arguments:
- features: bfloat16 [64, 512, 256], P(('grp', 'lat'), 'lon'), parts along dimension 0, may hold values from -6 to 6
- cotangent: bfloat16 [64, 512, 256], P(('grp', 'lat'), 'lon'), parts along dimension 0, may hold values from -6 to 6
- weights: bfloat16 [8, 256, 256], replicated, may hold values from -0.375 to 0.375
- coef_table: float32 [32, 8], replicated, may hold values from 0.05 to 4.5
- lat_index: int32 [32], P('lat'), may hold values from 0 to 31
- dir_ids: int32 [8], replicated, may hold values from 0 to 7, each once
Outputs:
- grad_features: bfloat16 [64, 512, 256], P(('grp', 'lat'), 'lon'), parts along dimension 0
- grad_weights: float32 [4096, 256], P(('grp', 'lat', 'lon')), parts along dimension 0
- grad_table: float32 [64, 8], P('grp'), parts along dimension 0
The draws below stay inside these ranges and needn't reach their ends.
There are 2 independent parts, one for each index of `grp`. The reference program is written for one: setup_inputs(seed, part) draws one part's arguments, and reference() takes and returns one part's arrays. A program takes and returns all parts, laid end to end along the dimension named above; an argument that names none is the same for every part. Nothing has to cross between parts.
Inputs may be any that keep to these rules, and one draw needn't show every extreme that they name: `dir_ids`: each of the 8 directions belongs to exactly one expert.
All inputs are finite; a program needn't handle non-finite values.
Results may differ from the reference program's by a relative error of at most 0.0047.
Values may be sent and summed in bfloat16 or wider, within the bound.
A program may use at most 64 MiB of HBM per device.

```python
import jax
import jax.numpy as jnp
from jax import lax

C = 256
REL = 8
NLAT = 32
NLON = 512


def cell_field(key, offset_scale, spread_lo, spread_hi):
    noise_key, offset_key, scale_key = jax.random.split(key, 3)
    shape = (NLAT, NLON, C)
    noise = jax.random.normal(noise_key, shape, jnp.float32)
    row_scale = jnp.exp(jax.random.uniform(scale_key, (NLAT, 1, 1), jnp.float32, jnp.log(spread_lo), jnp.log(spread_hi)))
    offset = offset_scale * jax.random.normal(offset_key, (C,), jnp.float32)
    values = jnp.clip(noise * row_scale + offset[None, None, :], -6.0, 6.0)
    return values.astype(jnp.bfloat16)


def draw_features(key, part):
    key = jax.random.fold_in(key, 11)
    return cell_field(key, 0.12, 1.0, 1.0)


def draw_cotangent(key, part):
    key = jax.random.fold_in(key, 13)
    return cell_field(key, 0.12, 1.0, 1.0)


def draw_coef_table(key, part):
    key = jax.random.fold_in(key, 7)
    column = jnp.arange(REL, dtype=jnp.float32) / (REL - 1)
    scales = 0.4 * 4.0 ** column
    values = jax.random.uniform(key, (NLAT, REL), jnp.float32, 0.5, 1.5)
    return values * scales[None, :]


def set_ends(drawn, stream_key, low, top_value):
    index_at = [jax.random.randint(jax.random.fold_in(stream_key, axis), (), 0, length) for axis, length in enumerate(drawn.shape)]
    longest = drawn.shape.index(max(drawn.shape))
    beside = index_at[:longest] + [(index_at[longest] + 1) % drawn.shape[longest]] + index_at[longest + 1:]
    return drawn.at[tuple(index_at)].set(low).at[tuple(beside)].set(top_value)


def centred(rng, shape, deviation, reach, held_as=jnp.bfloat16):
    entries = jax.random.normal(rng, shape, jnp.float32) * deviation
    return jnp.minimum(jnp.maximum(entries, -reach), reach).astype(held_as)


def setup_inputs(seed: int = 0, part: int = 0) -> dict:
    keys = jax.random.split(jax.random.key(seed), 7)
    own_keys = jax.random.split(jax.random.fold_in(keys[6], part), 7)
    features = draw_features(jax.random.fold_in(jax.random.fold_in(keys[6], part), 71), part)
    cotangent = draw_cotangent(jax.random.fold_in(jax.random.fold_in(keys[6], part), 71), part)
    weights = centred(keys[2], (REL, C, C), C ** -0.5, 0.375)
    coef_table = draw_coef_table(jax.random.fold_in(keys[6], 71), part)
    lat_index = set_ends(jax.random.randint(keys[4], (NLAT,), 0, NLAT), jax.random.fold_in(keys[4], 1), 0, NLAT - 1).astype(jnp.int32)
    dir_ids = jax.random.permutation(keys[5], REL).astype(jnp.int32)
    return dict(features=features, cotangent=cotangent, weights=weights, coef_table=coef_table, lat_index=lat_index, dir_ids=dir_ids)


LAT_STEPS = (-1, -1, -1, 0, 0, 1, 1, 1)
LON_STEPS = (-1, 0, 1, -1, 1, -1, 0, 1)
clip_norm = 512.0

def reference(features, cotangent, weights, coef_table, lat_index, dir_ids):
    lat_count, lon_count, latent = features.shape
    experts = weights.shape[0]
    padded = jnp.pad(features, ((1, 1), (0, 0), (0, 0)))
    padded = jnp.concatenate([padded[:, -1:], padded, padded[:, :1]], axis=1)
    row_coef = coef_table[lat_index]
    grad32 = cotangent.astype(jnp.float32)
    cotan_rows = grad32.reshape(lat_count * lon_count, latent)
    lat_table = jnp.array(LAT_STEPS, jnp.int32)
    lon_table = jnp.array(LON_STEPS, jnp.int32)

    def per_expert(spread, expert):
        direction = dir_ids[expert]
        anchor = (jnp.int32(1) + lat_table[direction], jnp.int32(1) + lon_table[direction], jnp.int32(0))
        neighbours = lax.dynamic_slice(padded, anchor, (lat_count, lon_count, latent)).reshape(lat_count * lon_count, latent)
        weight = weights[expert]
        preact = jnp.dot(neighbours, weight, preferred_element_type=jnp.float32)
        logistic = jax.nn.sigmoid(preact)
        activated = preact * logistic
        derivative = logistic * (1.0 + preact * (1.0 - logistic))
        row_sums = lax.optimization_barrier(jnp.sum((cotan_rows * activated).reshape(lat_count, lon_count * latent), axis=1))
        coef_rows = jnp.repeat(row_coef[:, expert], lon_count)[:, None]
        pre_grad = (cotan_rows * coef_rows * derivative).astype(jnp.bfloat16)
        weight_grad = jnp.dot(neighbours.T, pre_grad, preferred_element_type=jnp.float32)
        returned = jnp.dot(pre_grad, weight.T, preferred_element_type=jnp.float32).reshape(lat_count, lon_count, latent)
        current = lax.dynamic_slice(spread, anchor, (lat_count, lon_count, latent))
        spread = lax.dynamic_update_slice(spread, current + returned, anchor)
        return (spread, (weight_grad, row_sums))
    start = jnp.zeros((lat_count + 2, lon_count + 2, latent), jnp.float32)
    spread, (weight_grads, row_sums) = lax.scan(per_expert, start, jnp.arange(experts, dtype=jnp.int32))
    spread = spread.at[:, 1].add(spread[:, lon_count + 1]).at[:, lon_count].add(spread[:, 0])
    grad_features = (grad32 + spread[1:lat_count + 1, 1:lon_count + 1]).astype(jnp.bfloat16)
    table_sum = jnp.zeros((lat_count, experts), jnp.float32).at[lat_index].add(row_sums.T)
    weight_sum = weight_grads.reshape(experts * latent, latent)
    squares = jnp.sum(weight_sum * weight_sum) + jnp.sum(table_sum * table_sum)
    factor = jnp.minimum(1.0, clip_norm / jnp.sqrt(squares + 1e-06))
    return (grad_features, factor * weight_sum, factor * table_sum)
```

```python
import functools

import jax
import jax.numpy as jnp
from jax import lax
from jax.experimental import pallas as pl
from jax.experimental.pallas import tpu as pltpu
from jax.sharding import PartitionSpec as P

MESH = pl.DeviceIdType.MESH
F32, BF16 = jnp.float32, jnp.bfloat16
DIRS = tuple((a, b) for a in (-1, 0, 1) for b in (-1, 0, 1) if (a, b) != (0, 0))


def fused(nlat, nlon, feat, cot, wts, coef, lidx, dirs, gf, gw, gt,
          P, CT, W, F, S, PG, WG, CR, XS, XR, KP, ZS, ZR, A, T, TR, Q, QR, OH,
          CS, CV, RS, RV, G,
          lsem, hs, hr, cs, cr, xs, xr, zs, zr, ts, tr, qs, qr, gs, gr):
    lat = lax.axis_index("lat")
    lon = lax.axis_index("lon")
    size = nlat * nlon
    me = lat * nlon + lon
    core = lon % 2
    side = lon // 2
    rows, cols, ch = cot.shape

    def rcopy(src, dst, ssem, rsem, to_lat, to_lon):
        return pltpu.make_async_remote_copy(
            src_ref=src, dst_ref=dst, send_sem=ssem, recv_sem=rsem,
            device_id={"lat": to_lat, "lon": to_lon}, device_id_type=MESH)

    loc = [pltpu.make_async_copy(feat, P.at[pl.ds(1, rows), pl.ds(16, cols)], lsem.at[0]),
           pltpu.make_async_copy(cot, CT, lsem.at[1]),
           pltpu.make_async_copy(wts, W, lsem.at[2])]
    for c in loc:
        c.start()

    barrier = pltpu.get_barrier_semaphore()

    def greet(j, _):
        o = (me + j) % size
        pl.semaphore_signal(barrier, inc=1, device_id={"lat": o // nlon, "lon": o % nlon},
                            device_id_type=MESH)
        return 0
    lax.fori_loop(1, size, greet, 0)

    @pl.when(lat == 0)
    def _():
        P[0] = jnp.zeros(P.shape[1:], BF16)

    @pl.when(lat == nlat - 1)
    def _():
        P[rows + 1] = jnp.zeros(P.shape[1:], BF16)

    lane = lax.broadcasted_iota(jnp.int32, (1, OH.shape[1]), 1)
    for i in range(rows):
        OH[i:i + 1, :] = (lane == lidx[i]).astype(F32)

    loc[0].wait()
    pl.semaphore_wait(barrier, size - 1)

    def halo(m):
        a, b = DIRS[m]
        srow = {-1: 1, 0: pl.ds(1, rows), 1: rows}[a]
        drow = {-1: rows + 1, 0: pl.ds(1, rows), 1: 0}[a]
        scol = {-1: pl.ds(16, 16), 0: pl.ds(16, cols), 1: pl.ds(cols, 16)}[b]
        dcol = {-1: pl.ds(16 + cols, 16), 0: pl.ds(16, cols), 1: pl.ds(0, 16)}[b]
        return rcopy(P.at[srow, scol], P.at[drow, dcol], hs.at[m], hr.at[m],
                     lat + a, (lon + b + nlon) % nlon)

    def where_ok(pos, fn):
        pl.when(jnp.logical_and(pos >= 0, pos < nlat))(fn)

    for m, (a, b) in enumerate(DIRS):
        where_ok(lat + a, lambda m=m: halo(m).start())
    for m, (a, b) in enumerate(DIRS):
        where_ok(lat - a, lambda m=m: halo(m).wait_recv())

    for r in range(rows + 2):
        F[r] = P[r].astype(F32)
        S[rows + 2 + r] = P[r, 16:16 + cols]
    for r in range(rows + 2):
        S[r] = F[r, 15:15 + cols].astype(BF16)
        S[2 * (rows + 2) + r] = F[r, 17:17 + cols].astype(BF16)
    loc[1].wait()
    loc[2].wait()

    def ccopy(i):
        return rcopy(WG.at[i, 1 - core], CR.at[i], cs.at[i], cr.at[i], lat, lon + 1 - 2 * core)

    def xcopy(s):
        return rcopy(XS.at[s], XR.at[s], xs.at[s], xr.at[s], lat, (lon + 2) % nlon)

    def zcopy(s):
        return rcopy(ZS.at[s], ZR.at[s], zs.at[s], zr.at[s], (lat + 1 + s) % nlat, lon)

    def stage_x(s):
        ccopy(2 * s).wait_recv()
        ccopy(2 * s + 1).wait_recv()
        o = 2 * s + 1 - side
        k = 2 * s + side
        XS[s] = (WG[o, core] + CR[o]).astype(BF16)
        xcopy(s).start()
        KP[s] = WG[k, core] + CR[k]

    def stage_z(s):
        xcopy(s).wait_recv()
        ZS[s] = (KP[s] + XR[s].astype(F32)).astype(BF16)
        zcopy(s).start()

    def step(i, _):
        s = i // 2
        e = 2 * ((lat + 1 + s) % nlat) + i % 2
        k = dirs[e]
        kp = k + (k >= 4).astype(jnp.int32)
        base = (kp % 3) * (rows + 2) + kp // 3
        w = W[e]
        sums = []
        for c in range(rows // 2):
            x = S[pl.ds(base + 2 * c, 2)].reshape(2 * cols, ch)
            pre2 = jnp.dot(x, w, preferred_element_type=F32)
            for h in range(2):
                r = 2 * c + h
                pre = pre2[h * cols:(h + 1) * cols]
                sg = 0.5 * jnp.tanh(0.5 * pre) + 0.5
                act = pre * sg
                der = sg + act * (1.0 - sg)
                g = CT[r].astype(F32)
                sums.append(jnp.sum(g * act, axis=0, keepdims=True))
                PG[e, r] = (g * coef[lidx[r], e] * der).astype(BF16)
        wg = lax.dot_general(S[pl.ds(base, rows)].reshape(rows * cols, ch),
                             PG[e].reshape(rows * cols, ch),
                             (((0,), (0,)), ((), ())), preferred_element_type=F32)
        WG[i] = wg.reshape(2, ch // 2, ch)
        ccopy(i).start()
        rsum = jnp.sum(jnp.concatenate(sums, axis=0), axis=1, keepdims=True)
        T[pl.ds(e, 1), :] = jnp.sum(rsum * OH[...], axis=0, keepdims=True)

        @pl.when(jnp.logical_and(i % 2 == 0, i >= 2))
        def _():
            stage_x(i // 2 - 1)

        @pl.when(jnp.logical_and(i % 2 == 1, i >= 3))
        def _():
            stage_z((i - 3) // 2)
        return 0

    lax.fori_loop(0, 2 * nlat, step, 0)

    def tcopy(j):
        o = (me + j) % size
        return rcopy(T, TR.at[me], ts.at[j], tr.at[j], o // nlon, o % nlon)

    def qcopy(j):
        o = (me + j) % size
        return rcopy(Q, QR.at[me], qs.at[j], qr.at[j], o // nlon, o % nlon)

    def each(fn):
        def run(j, _):
            fn(j)
            return 0
        lax.fori_loop(1, size, run, 0)

    each(lambda j: tcopy(j).start())
    TR[me] = T[...]

    def expert_of(k):
        e = jnp.int32(0)
        for i in range(2 * nlat):
            e = jnp.where(dirs[i] == k, jnp.int32(i), e)
        return e

    def back(b):
        ks = [k for k in range(8) if DIRS[k][1] == b]
        first = True
        A[b + 1, 0:1, :, :] = jnp.zeros((1,) + A.shape[2:], F32)
        A[b + 1, rows + 1:rows + 2, :, :] = jnp.zeros((1,) + A.shape[2:], F32)
        if b == 0:
            A[b + 1, rows:rows + 1, :, :] = jnp.zeros((1,) + A.shape[2:], F32)
        for k in ks:
            a = DIRS[k][0]
            e = expert_of(k)
            ret = lax.dot_general(PG[e].reshape(rows * cols, ch), W[e],
                                  (((1,), (1,)), ((), ())), preferred_element_type=F32)
            ret = ret.reshape(rows, cols, ch)
            if first:
                A[b + 1, 1 + a:1 + a + rows, 8:8 + cols, :] = ret
                if b != 0:
                    A[b + 1, rows:rows + 1, 8:8 + cols, :] = jnp.zeros((1, cols, ch), F32)
                first = False
            else:
                A[b + 1, 1 + a:1 + a + rows, 8:8 + cols, :] += ret

    def colcopy(side_i, a):
        m = side_i * 3 + a + 1
        b = 2 * side_i - 1
        return rcopy(CS.at[side_i], CV.at[m], gs.at[m], gr.at[m],
                     lat + a, (lon + b + nlon) % nlon)

    def rowcopy(a):
        m = 6 + (a + 1) // 2
        return rcopy(RS.at[(a + 1) // 2], RV.at[(a + 1) // 2], gs.at[m], gr.at[m], lat + a, lon)

    back(-1)
    for r in range(rows + 2):
        CS[0, r:r + 1, :] = A[0, r, 8:9, :]
    CS[0, rows + 2:16, :] = jnp.zeros((14 - rows, ch), F32)
    for a in (-1, 0, 1):
        where_ok(lat + a, lambda a=a: colcopy(0, a).start())
    stage_x(nlat - 1)
    back(1)
    for r in range(rows + 2):
        CS[1, r:r + 1, :] = A[2, r, 7 + cols:8 + cols, :]
    CS[1, rows + 2:16, :] = jnp.zeros((14 - rows, ch), F32)
    for a in (-1, 0, 1):
        where_ok(lat + a, lambda a=a: colcopy(1, a).start())
    back(0)
    for h, r in ((0, 0), (1, rows + 1)):
        RS[h] = (A[1, r, 8:8 + cols] + A[0, r, 9:9 + cols] + A[2, r, 7:7 + cols]).astype(BF16)
    for a in (-1, 1):
        where_ok(lat + a, lambda a=a: rowcopy(a).start())

    xcopy(nlat - 1).wait_recv()
    total = KP[nlat - 1] + XR[nlat - 1].astype(F32)
    for s in range(nlat - 1):
        zcopy(s).wait_recv()
        total = total + ZR[s].astype(F32)
    G[...] = total
    sq = jnp.sum((total * total).reshape(ch // 16, 8, ch), axis=0)
    Q[...] = sq[:, :128] + sq[:, 128:]
    each(lambda j: qcopy(j).start())
    QR[me] = Q[...]

    for side_i in (0, 1):
        col = (8 + cols, 7)[side_i]
        acc = 2 * side_i
        colcopy(side_i, 0).wait_recv()
        for i in range(rows):
            A[acc, 1 + i, col:col + 1, :] = CV[side_i * 3 + 1, 1 + i:2 + i, :]

        def from_below(side_i=side_i, acc=acc, col=col):
            colcopy(side_i, -1).wait_recv()
            A[acc, rows, col:col + 1, :] += CV[side_i * 3, 0:1, :]

        def from_above(side_i=side_i, acc=acc, col=col):
            colcopy(side_i, 1).wait_recv()
            A[acc, 1, col:col + 1, :] += CV[side_i * 3 + 2, rows + 1:rows + 2, :]
        where_ok(lat + 1, from_below)
        where_ok(lat - 1, from_above)

    def row_below():
        rowcopy(-1).wait_recv()
        A[1, rows, 8:8 + cols, :] += RV[0].astype(F32)

    def row_above():
        rowcopy(1).wait_recv()
        A[1, 1, 8:8 + cols, :] += RV[1].astype(F32)
    where_ok(lat + 1, row_below)
    where_ok(lat - 1, row_above)
    for i in range(rows):
        gf[i] = (CT[i].astype(F32) + A[1, 1 + i, 8:8 + cols] + A[0, 1 + i, 9:9 + cols]
                 + A[2, 1 + i, 7:7 + cols]).astype(BF16)

    each(lambda j: tcopy(j).wait_recv())
    table = TR[0]
    for j in range(1, size):
        table = table + TR[j]
    each(lambda j: qcopy(j).wait_recv())
    sq = QR[0]
    for j in range(1, size):
        sq = sq + QR[j]
    squares = jnp.sum(sq, keepdims=True) + jnp.sum(table * table, keepdims=True)
    factor = jnp.minimum(1.0, 512.0 / jnp.sqrt(squares + 1e-06))
    gw[...] = G[...] * factor
    scaled = table * factor
    wide = jnp.concatenate([scaled, jnp.zeros((120, scaled.shape[1]), F32)], axis=0)
    gt[...] = wide.T[:gt.shape[0], :gt.shape[1]]

    for m, (a, b) in enumerate(DIRS):
        where_ok(lat + a, lambda m=m: halo(m).wait_send())
    for i in range(2 * nlat):
        ccopy(i).wait_send()
    for s in range(nlat):
        xcopy(s).wait_send()
    for s in range(nlat - 1):
        zcopy(s).wait_send()
    each(lambda j: tcopy(j).wait_send())
    each(lambda j: qcopy(j).wait_send())
    for side_i in (0, 1):
        for a in (-1, 0, 1):
            where_ok(lat + a, lambda side_i=side_i, a=a: colcopy(side_i, a).wait_send())
    for a in (-1, 1):
        where_ok(lat + a, lambda a=a: rowcopy(a).wait_send())


def fused_body(features, cotangent, weights, coef_table, lat_index, dir_ids):
    nlat, nlon = lax.axis_size("lat"), lax.axis_size("lon")
    rows, cols, ch = features.shape
    experts = weights.shape[0]
    table_rows = coef_table.shape[0]
    lanes = -(-table_rows // 128) * 128
    size = nlat * nlon
    half = ch // 2
    V = pltpu.VMEM
    D = pltpu.SemaphoreType.DMA
    any_spec = pl.BlockSpec(memory_space=pl.ANY)
    smem = pl.BlockSpec(memory_space=pltpu.SMEM)
    vmem = pl.BlockSpec(memory_space=pltpu.VMEM)
    cells = rows * cols
    return pl.pallas_call(
        functools.partial(fused, nlat, nlon),
        out_shape=(jax.ShapeDtypeStruct(features.shape, BF16),
                   jax.ShapeDtypeStruct((half, ch), F32),
                   jax.ShapeDtypeStruct((table_rows, experts), F32)),
        in_specs=[any_spec] * 3 + [smem] * 3,
        out_specs=(vmem, vmem, vmem),
        scratch_shapes=[
            V((rows + 2, cols + 32, ch), BF16),
            V((rows, cols, ch), BF16),
            V((experts, ch, ch), BF16),
            V((rows + 2, cols + 32, ch), F32),
            V((3 * (rows + 2), cols, ch), BF16),
            V((experts, rows, cols, ch), BF16),
            V((experts, 2, half, ch), F32),
            V((experts, half, ch), F32),
            V((nlat, half, ch), BF16),
            V((nlat, half, ch), BF16),
            V((nlat, half, ch), F32),
            V((nlat - 1, half, ch), BF16),
            V((nlat - 1, half, ch), BF16),
            V((3, rows + 2, cols + 16, ch), F32),
            V((experts, lanes), F32),
            V((size, experts, lanes), F32),
            V((8, 128), F32),
            V((size, 8, 128), F32),
            V((rows, lanes), F32),
            V((2, 16, ch), F32),
            V((6, 16, ch), F32),
            V((2, cols, ch), BF16),
            V((2, cols, ch), BF16),
            V((half, ch), F32),
            D((3,)), D((8,)), D((8,)), D((experts,)), D((experts,)),
            D((nlat,)), D((nlat,)), D((nlat,)), D((nlat,)),
            D((size,)), D((size,)), D((size,)), D((size,)), D((8,)), D((8,)),
        ],
        compiler_params=pltpu.CompilerParams(
            collective_id=0, has_side_effects=True, vmem_limit_bytes=48 * 1024 * 1024),
        cost_estimate=pl.CostEstimate(flops=6 * experts * cells * ch * ch,
                                      bytes_accessed=4 * 1024 * 1024,
                                      transcendentals=experts * cells * ch),
        name="relation_backward",
    )(features, cotangent, weights, coef_table, lat_index, dir_ids)


STEP_PAIRS = ((-1, -1), (-1, 0), (-1, 1), (0, -1), (0, 1), (1, -1), (1, 0), (1, 1))
clip_norm = 512.0


def with_halo(block, sides, width):
    for axis, dim in sides:
        count = lax.axis_size(axis)
        forward = [(i, i + 1) for i in range(count - 1)]
        forward.append((count - 1, 0))
        backward = [(target, source) for source, target in forward]
        low = lax.ppermute(
            lax.slice_in_dim(block, block.shape[dim] - width, None, axis=dim), axis, forward
        )
        high = lax.ppermute(lax.slice_in_dim(block, 0, width, axis=dim), axis, backward)
        block = jnp.concatenate([low, block, high], axis=dim)
    return block


def body(features, cotangent, weights, coef_table, lat_index, dir_ids):
    lat_rows, lon_cols, latent = features.shape
    experts = weights.shape[0]
    global_rows = coef_table.shape[0]
    lat_size = lax.axis_size("lat")
    lat_pos = lax.axis_index("lat")
    keep_top = (lat_pos > 0).astype(jnp.float32)
    keep_bottom = (lat_pos < lat_size - 1).astype(jnp.float32)
    padded = with_halo(features, (("lat", 0), ("lon", 1)), 1)
    padded = jnp.concatenate(
        [
            padded[:1] * keep_top.astype(jnp.bfloat16),
            padded[1:-1],
            padded[-1:] * keep_bottom.astype(jnp.bfloat16),
        ],
        axis=0,
    )
    shifted = jnp.stack(
        [
            padded[1 + lat_step : 1 + lat_step + lat_rows, 1 + lon_step : 1 + lon_step + lon_cols]
            for lat_step, lon_step in STEP_PAIRS
        ]
    )
    neighbours = jnp.take(shifted, dir_ids, axis=0).reshape(experts, lat_rows * lon_cols, latent)
    preact = jnp.einsum("epc,ecd->epd", neighbours, weights, preferred_element_type=jnp.float32)
    logistic = jax.nn.sigmoid(preact)
    activated = (preact * logistic).reshape(experts, lat_rows, lon_cols, latent)
    derivative = (logistic * (1.0 + preact * (1.0 - logistic))).reshape(
        experts, lat_rows, lon_cols, latent
    )
    picker = (lat_index[:, None] == jnp.arange(global_rows, dtype=jnp.int32)[None, :]).astype(
        jnp.float32
    )
    row_coef = jnp.dot(picker, coef_table, precision=lax.Precision.HIGHEST)
    grad32 = cotangent.astype(jnp.float32)
    row_sums = jnp.sum(grad32[None] * activated, axis=(2, 3))
    table_part = jnp.dot(picker.T, row_sums.T, precision=lax.Precision.HIGHEST)
    pre_grad = (grad32[None] * row_coef.T[:, :, None, None] * derivative).astype(jnp.bfloat16)
    pre_grad = pre_grad.reshape(experts, lat_rows * lon_cols, latent)
    weight_part = jnp.einsum(
        "epc,epd->ecd", neighbours, pre_grad, preferred_element_type=jnp.float32
    ).reshape(experts * latent, latent)
    returned = jnp.einsum(
        "epd,ecd->epc", pre_grad, weights, preferred_element_type=jnp.float32
    ).reshape(experts, lat_rows, lon_cols, latent)
    inverse = jnp.argsort(dir_ids)
    by_direction = jnp.take(returned, inverse, axis=0)
    spread = jnp.zeros((lat_rows + 2, lon_cols + 2, latent), jnp.float32)
    for index, (lat_step, lon_step) in enumerate(STEP_PAIRS):
        spread = spread + jnp.pad(
            by_direction[index],
            ((1 + lat_step, 1 - lat_step), (1 + lon_step, 1 - lon_step), (0, 0)),
        )
    rimmed = with_halo(spread, (("lat", 0), ("lon", 1)), 1)
    folded = rimmed[:, 2 : lon_cols + 2]
    folded = folded.at[:, 0].add(rimmed[:, 0]).at[:, lon_cols - 1].add(rimmed[:, lon_cols + 3])
    interior = folded[2 : lat_rows + 2]
    interior = (
        interior.at[0]
        .add(folded[0] * keep_top)
        .at[lat_rows - 1]
        .add(folded[lat_rows + 3] * keep_bottom)
    )
    grad_features = (grad32 + interior).astype(jnp.bfloat16)
    table_grad = lax.psum(table_part, ("lat", "lon"))
    weight_shard = lax.psum_scatter(weight_part, ("lat", "lon"), scatter_dimension=0, tiled=True)
    shard_squares = lax.psum(jnp.sum(weight_shard * weight_shard), ("lat", "lon"))
    squares = shard_squares + jnp.sum(table_grad * table_grad)
    factor = jnp.minimum(1.0, clip_norm / jnp.sqrt(squares + 1e-06))
    return (grad_features, factor * weight_shard, factor * table_grad)


def solution(mesh):
    in_specs = (
        P(("grp", "lat"), "lon", None),
        P(("grp", "lat"), "lon", None),
        P(),
        P(),
        P("lat"),
        P(),
    )
    out_specs = (P(("grp", "lat"), "lon", None), P(("grp", "lat", "lon"), None), P("grp", None))
    fits = mesh.shape["lat"] == 4 and mesh.shape["lon"] == 4
    chosen = fused_body if fits else body
    return jax.shard_map(chosen, mesh=mesh, in_specs=in_specs, out_specs=out_specs, check_vma=False)
```

```python
import functools

import jax
import jax.numpy as jnp
from jax import lax
from jax.experimental import pallas as pl
from jax.experimental.pallas import tpu as pltpu
from jax.sharding import PartitionSpec as P

MESH = pl.DeviceIdType.MESH
F32, BF16 = jnp.float32, jnp.bfloat16
DIRS = tuple((a, b) for a in (-1, 0, 1) for b in (-1, 0, 1) if (a, b) != (0, 0))


def fused(nlat, nlon, feat, cot, wts, coef, lidx, dirs, gf, gw, gt,
          P, CT, W, F, S, PG, WG, CR, XS, XR, KP, ZS, ZR, A, T, TR, Q, QR, OH,
          CS, CV, RS, RV, G,
          lsem, hs, hr, cs, cr, xs, xr, zs, zr, ts, tr, qs, qr, gs, gr):
    lat = lax.axis_index("lat")
    lon = lax.axis_index("lon")
    size = nlat * nlon
    me = lat * nlon + lon
    core = lon % 2
    side = lon // 2
    rows, cols, ch = cot.shape

    def rcopy(src, dst, ssem, rsem, to_lat, to_lon):
        return pltpu.make_async_remote_copy(
            src_ref=src, dst_ref=dst, send_sem=ssem, recv_sem=rsem,
            device_id={"lat": to_lat, "lon": to_lon}, device_id_type=MESH)

    loc = [pltpu.make_async_copy(feat, P.at[pl.ds(1, rows), pl.ds(16, cols)], lsem.at[0]),
           pltpu.make_async_copy(cot, CT, lsem.at[1]),
           pltpu.make_async_copy(wts, W, lsem.at[2])]
    for c in loc:
        c.start()

    barrier = pltpu.get_barrier_semaphore()

    def greet(j, _):
        o = (me + j) % size
        pl.semaphore_signal(barrier, inc=1, device_id={"lat": o // nlon, "lon": o % nlon},
                            device_id_type=MESH)
        return 0
    lax.fori_loop(1, size, greet, 0)

    @pl.when(lat == 0)
    def _():
        P[0] = jnp.zeros(P.shape[1:], BF16)

    @pl.when(lat == nlat - 1)
    def _():
        P[rows + 1] = jnp.zeros(P.shape[1:], BF16)

    lane = lax.broadcasted_iota(jnp.int32, (1, OH.shape[1]), 1)
    for i in range(rows):
        OH[i:i + 1, :] = (lane == lidx[i]).astype(F32)

    loc[0].wait()
    pl.semaphore_wait(barrier, size - 1)

    def halo(m):
        a, b = DIRS[m]
        srow = {-1: 1, 0: pl.ds(1, rows), 1: rows}[a]
        drow = {-1: rows + 1, 0: pl.ds(1, rows), 1: 0}[a]
        scol = {-1: pl.ds(16, 16), 0: pl.ds(16, cols), 1: pl.ds(cols, 16)}[b]
        dcol = {-1: pl.ds(16 + cols, 16), 0: pl.ds(16, cols), 1: pl.ds(0, 16)}[b]
        return rcopy(P.at[srow, scol], P.at[drow, dcol], hs.at[m], hr.at[m],
                     lat + a, (lon + b + nlon) % nlon)

    def where_ok(pos, fn):
        pl.when(jnp.logical_and(pos >= 0, pos < nlat))(fn)

    for m, (a, b) in enumerate(DIRS):
        where_ok(lat + a, lambda m=m: halo(m).start())
    for m, (a, b) in enumerate(DIRS):
        where_ok(lat - a, lambda m=m: halo(m).wait_recv())

    for r in range(rows + 2):
        F[r] = P[r].astype(F32)
        S[rows + 2 + r] = P[r, 16:16 + cols]
    for r in range(rows + 2):
        S[r] = F[r, 15:15 + cols].astype(BF16)
        S[2 * (rows + 2) + r] = F[r, 17:17 + cols].astype(BF16)
    loc[1].wait()
    loc[2].wait()

    def ccopy(i):
        return rcopy(WG.at[i, 1 - core], CR.at[i], cs.at[i], cr.at[i], lat, lon + 1 - 2 * core)

    def xcopy(s):
        return rcopy(XS.at[s], XR.at[s], xs.at[s], xr.at[s], lat, (lon + 2) % nlon)

    def zcopy(s):
        return rcopy(ZS.at[s], ZR.at[s], zs.at[s], zr.at[s], (lat + 1 + s) % nlat, lon)

    def stage_x(s):
        ccopy(2 * s).wait_recv()
        ccopy(2 * s + 1).wait_recv()
        o = 2 * s + 1 - side
        k = 2 * s + side
        XS[s] = (WG[o, core] + CR[o]).astype(BF16)
        xcopy(s).start()
        KP[s] = WG[k, core] + CR[k]

    def stage_z(s):
        xcopy(s).wait_recv()
        ZS[s] = (KP[s] + XR[s].astype(F32)).astype(BF16)
        zcopy(s).start()

    def step(i, _):
        s = i // 2
        e = 2 * ((lat + 1 + s) % nlat) + i % 2
        k = dirs[e]
        kp = k + (k >= 4).astype(jnp.int32)
        base = (kp % 3) * (rows + 2) + kp // 3
        w = W[e]
        sums = []
        for c in range(rows // 2):
            x = S[pl.ds(base + 2 * c, 2)].reshape(2 * cols, ch)
            pre2 = jnp.dot(x, w, preferred_element_type=F32)
            for h in range(2):
                r = 2 * c + h
                pre = pre2[h * cols:(h + 1) * cols]
                sg = 0.5 * jnp.tanh(0.5 * pre) + 0.5
                act = pre * sg
                der = sg + act * (1.0 - sg)
                g = CT[r].astype(F32)
                sums.append(jnp.sum(g * act, axis=0, keepdims=True))
                PG[e, r] = (g * coef[e, lidx[r]] * der).astype(BF16)
        wg = lax.dot_general(S[pl.ds(base, rows)].reshape(rows * cols, ch),
                             PG[e].reshape(rows * cols, ch),
                             (((0,), (0,)), ((), ())), preferred_element_type=F32)
        WG[i] = wg.reshape(2, ch // 2, ch)
        ccopy(i).start()
        rsum = jnp.sum(jnp.concatenate(sums, axis=0), axis=1, keepdims=True)
        T[pl.ds(e, 1), :] = jnp.sum(rsum * OH[...], axis=0, keepdims=True)

        @pl.when(jnp.logical_and(i % 2 == 0, i >= 2))
        def _():
            stage_x(i // 2 - 1)

        @pl.when(jnp.logical_and(i % 2 == 1, i >= 5))
        def _():
            stage_z((i - 5) // 2)
        return 0

    lax.fori_loop(0, 2 * nlat, step, 0)

    def tcopy(j):
        o = (me + j) % size
        return rcopy(T, TR.at[me], ts.at[j], tr.at[j], o // nlon, o % nlon)

    def qcopy(j):
        o = (me + j) % size
        return rcopy(Q, QR.at[me], qs.at[j], qr.at[j], o // nlon, o % nlon)

    def each(fn):
        def run(j, _):
            fn(j)
            return 0
        lax.fori_loop(1, size, run, 0)

    each(lambda j: tcopy(j).start())
    TR[me] = T[...]

    def expert_of(k):
        e = jnp.int32(0)
        for i in range(2 * nlat):
            e = jnp.where(dirs[i] == k, jnp.int32(i), e)
        return e

    def back(b):
        ks = [k for k in range(8) if DIRS[k][1] == b]
        first = True
        A[b + 1, 0:1, :, :] = jnp.zeros((1,) + A.shape[2:], F32)
        A[b + 1, rows + 1:rows + 2, :, :] = jnp.zeros((1,) + A.shape[2:], F32)
        if b == 0:
            A[b + 1, rows:rows + 1, :, :] = jnp.zeros((1,) + A.shape[2:], F32)
        for k in ks:
            a = DIRS[k][0]
            e = expert_of(k)
            ret = lax.dot_general(PG[e].reshape(rows * cols, ch), W[e],
                                  (((1,), (1,)), ((), ())), preferred_element_type=F32)
            ret = ret.reshape(rows, cols, ch)
            if first:
                A[b + 1, 1 + a:1 + a + rows, 8:8 + cols, :] = ret
                if b != 0:
                    A[b + 1, rows:rows + 1, 8:8 + cols, :] = jnp.zeros((1, cols, ch), F32)
                first = False
            else:
                A[b + 1, 1 + a:1 + a + rows, 8:8 + cols, :] += ret

    def colcopy(side_i, a):
        m = side_i * 3 + a + 1
        b = 2 * side_i - 1
        return rcopy(CS.at[side_i], CV.at[m], gs.at[m], gr.at[m],
                     lat + a, (lon + b + nlon) % nlon)

    def rowcopy(a):
        m = 6 + (a + 1) // 2
        return rcopy(RS.at[(a + 1) // 2], RV.at[(a + 1) // 2], gs.at[m], gr.at[m], lat + a, lon)

    back(-1)
    for r in range(rows + 2):
        CS[0, r:r + 1, :] = A[0, r, 8:9, :]
    CS[0, rows + 2:16, :] = jnp.zeros((14 - rows, ch), F32)
    for a in (-1, 0, 1):
        where_ok(lat + a, lambda a=a: colcopy(0, a).start())
    stage_x(nlat - 1)
    back(1)
    for r in range(rows + 2):
        CS[1, r:r + 1, :] = A[2, r, 7 + cols:8 + cols, :]
    CS[1, rows + 2:16, :] = jnp.zeros((14 - rows, ch), F32)
    for a in (-1, 0, 1):
        where_ok(lat + a, lambda a=a: colcopy(1, a).start())
    stage_z(nlat - 2)
    back(0)
    for h, r in ((0, 0), (1, rows + 1)):
        RS[h] = (A[1, r, 8:8 + cols] + A[0, r, 9:9 + cols] + A[2, r, 7:7 + cols]).astype(BF16)
    for a in (-1, 1):
        where_ok(lat + a, lambda a=a: rowcopy(a).start())

    xcopy(nlat - 1).wait_recv()
    total = KP[nlat - 1] + XR[nlat - 1].astype(F32)
    for s in range(nlat - 1):
        zcopy(s).wait_recv()
        total = total + ZR[s].astype(F32)
    G[...] = total
    sq = jnp.sum((total * total).reshape(ch // 16, 8, ch), axis=0)
    Q[...] = sq[:, :128] + sq[:, 128:]
    each(lambda j: qcopy(j).start())
    QR[me] = Q[...]

    for side_i in (0, 1):
        col = (8 + cols, 7)[side_i]
        acc = 2 * side_i
        colcopy(side_i, 0).wait_recv()
        for i in range(rows):
            A[acc, 1 + i, col:col + 1, :] = CV[side_i * 3 + 1, 1 + i:2 + i, :]

        def from_below(side_i=side_i, acc=acc, col=col):
            colcopy(side_i, -1).wait_recv()
            A[acc, rows, col:col + 1, :] += CV[side_i * 3, 0:1, :]

        def from_above(side_i=side_i, acc=acc, col=col):
            colcopy(side_i, 1).wait_recv()
            A[acc, 1, col:col + 1, :] += CV[side_i * 3 + 2, rows + 1:rows + 2, :]
        where_ok(lat + 1, from_below)
        where_ok(lat - 1, from_above)

    def row_below():
        rowcopy(-1).wait_recv()
        A[1, rows, 8:8 + cols, :] += RV[0].astype(F32)

    def row_above():
        rowcopy(1).wait_recv()
        A[1, 1, 8:8 + cols, :] += RV[1].astype(F32)
    where_ok(lat + 1, row_below)
    where_ok(lat - 1, row_above)
    for i in range(rows):
        gf[i] = (CT[i].astype(F32) + A[1, 1 + i, 8:8 + cols] + A[0, 1 + i, 9:9 + cols]
                 + A[2, 1 + i, 7:7 + cols]).astype(BF16)

    each(lambda j: tcopy(j).wait_recv())
    table = TR[0]
    for j in range(1, size):
        table = table + TR[j]
    each(lambda j: qcopy(j).wait_recv())
    sq = QR[0]
    for j in range(1, size):
        sq = sq + QR[j]
    squares = jnp.sum(sq, keepdims=True) + jnp.sum(table * table, keepdims=True)
    factor = jnp.minimum(1.0, 512.0 / jnp.sqrt(squares + 1e-06))
    gw[...] = G[...] * factor
    scaled = table * factor
    gt[...] = scaled[:, :gt.shape[1]]

    for m, (a, b) in enumerate(DIRS):
        where_ok(lat + a, lambda m=m: halo(m).wait_send())
    for i in range(2 * nlat):
        ccopy(i).wait_send()
    for s in range(nlat):
        xcopy(s).wait_send()
    for s in range(nlat - 1):
        zcopy(s).wait_send()
    each(lambda j: tcopy(j).wait_send())
    each(lambda j: qcopy(j).wait_send())
    for side_i in (0, 1):
        for a in (-1, 0, 1):
            where_ok(lat + a, lambda side_i=side_i, a=a: colcopy(side_i, a).wait_send())
    for a in (-1, 1):
        where_ok(lat + a, lambda a=a: rowcopy(a).wait_send())


def fused_body(features, cotangent, weights, coef_table, lat_index, dir_ids):
    nlat, nlon = lax.axis_size("lat"), lax.axis_size("lon")
    rows, cols, ch = features.shape
    experts = weights.shape[0]
    table_rows = coef_table.shape[0]
    lanes = -(-table_rows // 128) * 128
    size = nlat * nlon
    half = ch // 2
    V = pltpu.VMEM
    D = pltpu.SemaphoreType.DMA
    any_spec = pl.BlockSpec(memory_space=pl.ANY)
    smem = pl.BlockSpec(memory_space=pltpu.SMEM)
    vmem = pl.BlockSpec(memory_space=pltpu.VMEM)
    cells = rows * cols
    grad_features, grad_weights, grad_table = pl.pallas_call(
        functools.partial(fused, nlat, nlon),
        out_shape=(jax.ShapeDtypeStruct(features.shape, BF16),
                   jax.ShapeDtypeStruct((half, ch), F32),
                   jax.ShapeDtypeStruct((experts, table_rows), F32)),
        in_specs=[any_spec] * 3 + [smem] * 3,
        out_specs=(vmem, vmem, vmem),
        scratch_shapes=[
            V((rows + 2, cols + 32, ch), BF16),
            V((rows, cols, ch), BF16),
            V((experts, ch, ch), BF16),
            V((rows + 2, cols + 32, ch), F32),
            V((3 * (rows + 2), cols, ch), BF16),
            V((experts, rows, cols, ch), BF16),
            V((experts, 2, half, ch), F32),
            V((experts, half, ch), F32),
            V((nlat, half, ch), BF16),
            V((nlat, half, ch), BF16),
            V((nlat, half, ch), F32),
            V((nlat - 1, half, ch), BF16),
            V((nlat - 1, half, ch), BF16),
            V((3, rows + 2, cols + 16, ch), F32),
            V((experts, lanes), F32),
            V((size, experts, lanes), F32),
            V((8, 128), F32),
            V((size, 8, 128), F32),
            V((rows, lanes), F32),
            V((2, 16, ch), F32),
            V((6, 16, ch), F32),
            V((2, cols, ch), BF16),
            V((2, cols, ch), BF16),
            V((half, ch), F32),
            D((3,)), D((8,)), D((8,)), D((experts,)), D((experts,)),
            D((nlat,)), D((nlat,)), D((nlat,)), D((nlat,)),
            D((size,)), D((size,)), D((size,)), D((size,)), D((8,)), D((8,)),
        ],
        compiler_params=pltpu.CompilerParams(
            collective_id=0, has_side_effects=True, vmem_limit_bytes=62 * 1024 * 1024),
        cost_estimate=pl.CostEstimate(flops=6 * experts * cells * ch * ch,
                                      bytes_accessed=4 * 1024 * 1024,
                                      transcendentals=experts * cells * ch),
        name="relation_backward",
    )(features, cotangent, weights, coef_table.T, lat_index, dir_ids)
    return grad_features, grad_weights, grad_table.T


STEP_PAIRS = ((-1, -1), (-1, 0), (-1, 1), (0, -1), (0, 1), (1, -1), (1, 0), (1, 1))
clip_norm = 512.0


def with_halo(block, sides, width):
    for axis, dim in sides:
        count = lax.axis_size(axis)
        forward = [(i, i + 1) for i in range(count - 1)]
        forward.append((count - 1, 0))
        backward = [(target, source) for source, target in forward]
        low = lax.ppermute(
            lax.slice_in_dim(block, block.shape[dim] - width, None, axis=dim), axis, forward
        )
        high = lax.ppermute(lax.slice_in_dim(block, 0, width, axis=dim), axis, backward)
        block = jnp.concatenate([low, block, high], axis=dim)
    return block


def body(features, cotangent, weights, coef_table, lat_index, dir_ids):
    lat_rows, lon_cols, latent = features.shape
    experts = weights.shape[0]
    global_rows = coef_table.shape[0]
    lat_size = lax.axis_size("lat")
    lat_pos = lax.axis_index("lat")
    keep_top = (lat_pos > 0).astype(jnp.float32)
    keep_bottom = (lat_pos < lat_size - 1).astype(jnp.float32)
    padded = with_halo(features, (("lat", 0), ("lon", 1)), 1)
    padded = jnp.concatenate(
        [
            padded[:1] * keep_top.astype(jnp.bfloat16),
            padded[1:-1],
            padded[-1:] * keep_bottom.astype(jnp.bfloat16),
        ],
        axis=0,
    )
    shifted = jnp.stack(
        [
            padded[1 + lat_step : 1 + lat_step + lat_rows, 1 + lon_step : 1 + lon_step + lon_cols]
            for lat_step, lon_step in STEP_PAIRS
        ]
    )
    neighbours = jnp.take(shifted, dir_ids, axis=0).reshape(experts, lat_rows * lon_cols, latent)
    preact = jnp.einsum("epc,ecd->epd", neighbours, weights, preferred_element_type=jnp.float32)
    logistic = jax.nn.sigmoid(preact)
    activated = (preact * logistic).reshape(experts, lat_rows, lon_cols, latent)
    derivative = (logistic * (1.0 + preact * (1.0 - logistic))).reshape(
        experts, lat_rows, lon_cols, latent
    )
    picker = (lat_index[:, None] == jnp.arange(global_rows, dtype=jnp.int32)[None, :]).astype(
        jnp.float32
    )
    row_coef = jnp.dot(picker, coef_table, precision=lax.Precision.HIGHEST)
    grad32 = cotangent.astype(jnp.float32)
    row_sums = jnp.sum(grad32[None] * activated, axis=(2, 3))
    table_part = jnp.dot(picker.T, row_sums.T, precision=lax.Precision.HIGHEST)
    pre_grad = (grad32[None] * row_coef.T[:, :, None, None] * derivative).astype(jnp.bfloat16)
    pre_grad = pre_grad.reshape(experts, lat_rows * lon_cols, latent)
    weight_part = jnp.einsum(
        "epc,epd->ecd", neighbours, pre_grad, preferred_element_type=jnp.float32
    ).reshape(experts * latent, latent)
    returned = jnp.einsum(
        "epd,ecd->epc", pre_grad, weights, preferred_element_type=jnp.float32
    ).reshape(experts, lat_rows, lon_cols, latent)
    inverse = jnp.argsort(dir_ids)
    by_direction = jnp.take(returned, inverse, axis=0)
    spread = jnp.zeros((lat_rows + 2, lon_cols + 2, latent), jnp.float32)
    for index, (lat_step, lon_step) in enumerate(STEP_PAIRS):
        spread = spread + jnp.pad(
            by_direction[index],
            ((1 + lat_step, 1 - lat_step), (1 + lon_step, 1 - lon_step), (0, 0)),
        )
    rimmed = with_halo(spread, (("lat", 0), ("lon", 1)), 1)
    folded = rimmed[:, 2 : lon_cols + 2]
    folded = folded.at[:, 0].add(rimmed[:, 0]).at[:, lon_cols - 1].add(rimmed[:, lon_cols + 3])
    interior = folded[2 : lat_rows + 2]
    interior = (
        interior.at[0]
        .add(folded[0] * keep_top)
        .at[lat_rows - 1]
        .add(folded[lat_rows + 3] * keep_bottom)
    )
    grad_features = (grad32 + interior).astype(jnp.bfloat16)
    table_grad = lax.psum(table_part, ("lat", "lon"))
    weight_shard = lax.psum_scatter(weight_part, ("lat", "lon"), scatter_dimension=0, tiled=True)
    shard_squares = lax.psum(jnp.sum(weight_shard * weight_shard), ("lat", "lon"))
    squares = shard_squares + jnp.sum(table_grad * table_grad)
    factor = jnp.minimum(1.0, clip_norm / jnp.sqrt(squares + 1e-06))
    return (grad_features, factor * weight_shard, factor * table_grad)


def solution(mesh):
    in_specs = (
        P(("grp", "lat"), "lon", None),
        P(("grp", "lat"), "lon", None),
        P(),
        P(),
        P("lat"),
        P(),
    )
    out_specs = (P(("grp", "lat"), "lon", None), P(("grp", "lat", "lon"), None), P("grp", None))
    fits = mesh.shape["lat"] == 4 and mesh.shape["lon"] == 4
    chosen = fused_body if fits else body
    return jax.shard_map(chosen, mesh=mesh, in_specs=in_specs, out_specs=out_specs, check_vma=False)
```

```python
import functools

import jax
import jax.numpy as jnp
from jax import lax
from jax.experimental import pallas as pl
from jax.experimental.pallas import tpu as pltpu
from jax.sharding import PartitionSpec as P

MESH = pl.DeviceIdType.MESH
F32, BF16 = jnp.float32, jnp.bfloat16
DIRS = tuple((a, b) for a in (-1, 0, 1) for b in (-1, 0, 1) if (a, b) != (0, 0))


def fused(nlat, nlon, feat, cot, wts, coef, lidx, dirs, gf, gw, gt,
          P, CT, W, F, S, PG, WG, CR, XS, XR, KP, ZS, ZR, A, T, TR, Q, QR, OH,
          CS, CV, RS, RV, G,
          GF, lsem, hs, hr, cs, cr, xs, xr, zs, zr, ts, tr, qs, qr, gs, gr):
    lat = lax.axis_index("lat")
    lon = lax.axis_index("lon")
    size = nlat * nlon
    me = lat * nlon + lon
    core = lon % 2
    side = lon // 2
    rows, cols, ch = cot.shape

    def rcopy(src, dst, ssem, rsem, to_lat, to_lon):
        return pltpu.make_async_remote_copy(
            src_ref=src, dst_ref=dst, send_sem=ssem, recv_sem=rsem,
            device_id={"lat": to_lat, "lon": to_lon}, device_id_type=MESH)

    loc = [pltpu.make_async_copy(feat, P.at[pl.ds(1, rows), pl.ds(16, cols)], lsem.at[0]),
           pltpu.make_async_copy(cot, CT, lsem.at[1]),
           pltpu.make_async_copy(wts, W, lsem.at[2])]
    for c in loc:
        c.start()

    barrier = pltpu.get_barrier_semaphore()

    def greet(j, _):
        o = (me + j) % size
        pl.semaphore_signal(barrier, inc=1, device_id={"lat": o // nlon, "lon": o % nlon},
                            device_id_type=MESH)
        return 0
    lax.fori_loop(1, size, greet, 0)

    @pl.when(lat == 0)
    def _():
        P[0] = jnp.zeros(P.shape[1:], BF16)

    @pl.when(lat == nlat - 1)
    def _():
        P[rows + 1] = jnp.zeros(P.shape[1:], BF16)

    lane = lax.broadcasted_iota(jnp.int32, (1, OH.shape[1]), 1)
    for i in range(rows):
        OH[i:i + 1, :] = (lane == lidx[i]).astype(F32)

    loc[0].wait()
    pl.semaphore_wait(barrier, size - 1)

    def halo(m):
        a, b = DIRS[m]
        srow = {-1: 1, 0: pl.ds(1, rows), 1: rows}[a]
        drow = {-1: rows + 1, 0: pl.ds(1, rows), 1: 0}[a]
        scol = {-1: pl.ds(16, 16), 0: pl.ds(16, cols), 1: pl.ds(cols, 16)}[b]
        dcol = {-1: pl.ds(16 + cols, 16), 0: pl.ds(16, cols), 1: pl.ds(0, 16)}[b]
        return rcopy(P.at[srow, scol], P.at[drow, dcol], hs.at[m], hr.at[m],
                     lat + a, (lon + b + nlon) % nlon)

    def where_ok(pos, fn):
        pl.when(jnp.logical_and(pos >= 0, pos < nlat))(fn)

    for m, (a, b) in enumerate(DIRS):
        where_ok(lat + a, lambda m=m: halo(m).start())
    n = rows + 2
    for r in range(1, rows + 1):
        F[r, 16:16 + cols] = P[r, 16:16 + cols].astype(F32)
        S[n + r] = P[r, 16:16 + cols]
    for r in range(1, rows + 1):
        S[r, 16:cols] = F[r, 31:15 + cols].astype(BF16)
        S[2 * n + r, 0:cols - 16] = F[r, 17:1 + cols].astype(BF16)
    for m, (a, b) in enumerate(DIRS):
        where_ok(lat - a, lambda m=m: halo(m).wait_recv())
    for r in range(1, rows + 1):
        F[r, 0:16] = P[r, 0:16].astype(F32)
        F[r, 16 + cols:] = P[r, 16 + cols:].astype(F32)
    for r in (0, rows + 1):
        F[r] = P[r].astype(F32)
        S[n + r] = P[r, 16:16 + cols]
    for r in range(1, rows + 1):
        S[r, 0:16] = F[r, 15:31].astype(BF16)
        S[2 * n + r, cols - 16:cols] = F[r, 1 + cols:17 + cols].astype(BF16)
    for r in (0, rows + 1):
        S[r] = F[r, 15:15 + cols].astype(BF16)
        S[2 * n + r] = F[r, 17:17 + cols].astype(BF16)
    loc[1].wait()
    loc[2].wait()

    def ccopy(i):
        return rcopy(WG.at[i, 1 - core], CR.at[i], cs.at[i], cr.at[i], lat, lon + 1 - 2 * core)

    def xcopy(s):
        return rcopy(XS.at[s], XR.at[s], xs.at[s], xr.at[s], lat, (lon + 2) % nlon)

    def zcopy(s):
        return rcopy(ZS.at[s], ZR.at[s], zs.at[s], zr.at[s], (lat + 1 + s) % nlat, lon)

    def stage_x(s):
        ccopy(2 * s).wait_recv()
        ccopy(2 * s + 1).wait_recv()
        o = 2 * s + 1 - side
        k = 2 * s + side
        XS[s] = (WG[o, core] + CR[o]).astype(BF16)
        xcopy(s).start()
        KP[s] = WG[k, core] + CR[k]

    def stage_z(s):
        xcopy(s).wait_recv()
        ZS[s] = (KP[s] + XR[s].astype(F32)).astype(BF16)
        zcopy(s).start()

    def step(i, _):
        s = i // 2
        e = 2 * ((lat + 1 + s) % nlat) + i % 2
        k = dirs[e]
        kp = k + (k >= 4).astype(jnp.int32)
        base = (kp % 3) * (rows + 2) + kp // 3
        w = W[e] * jnp.asarray(0.5, BF16)
        sums = []
        for c in range(rows // 2):
            x = S[pl.ds(base + 2 * c, 2)].reshape(2 * cols, ch)
            pre2 = jnp.dot(x, w, preferred_element_type=F32)
            for h in range(2):
                r = 2 * c + h
                pre = pre2[h * cols:(h + 1) * cols]
                th = jnp.tanh(pre)
                up = 1.0 + th
                act = pre * up
                der = up + act * (1.0 - th)
                g = CT[r].astype(F32)
                sums.append(jnp.sum(g * act, axis=0, keepdims=True))
                PG[e, r] = (g * (0.5 * coef[e, lidx[r]]) * der).astype(BF16)
        wg = lax.dot_general(S[pl.ds(base, rows)].reshape(rows * cols, ch),
                             PG[e].reshape(rows * cols, ch),
                             (((0,), (0,)), ((), ())), preferred_element_type=F32)
        WG[i] = wg.reshape(2, ch // 2, ch)
        ccopy(i).start()
        rsum = jnp.sum(jnp.concatenate(sums, axis=0), axis=1, keepdims=True)
        T[pl.ds(e, 1), :] = jnp.sum(rsum * OH[...], axis=0, keepdims=True)

        @pl.when(jnp.logical_and(i % 2 == 0, i >= 2))
        def _():
            stage_x(i // 2 - 1)

        @pl.when(jnp.logical_and(i % 2 == 1, i >= 5))
        def _():
            stage_z((i - 5) // 2)
        return 0

    lax.fori_loop(0, 2 * nlat, step, 0)

    def tcopy(j):
        o = (me + j) % size
        return rcopy(T, TR.at[me], ts.at[j], tr.at[j], o // nlon, o % nlon)

    def qcopy(j):
        o = (me + j) % size
        return rcopy(Q, QR.at[me], qs.at[j], qr.at[j], o // nlon, o % nlon)

    def each(fn):
        def run(j, _):
            fn(j)
            return 0
        lax.fori_loop(1, size, run, 0)

    def expert_of(k):
        e = jnp.int32(0)
        for i in range(2 * nlat):
            e = jnp.where(dirs[i] == k, jnp.int32(i), e)
        return e

    def back(b):
        ks = [k for k in range(8) if DIRS[k][1] == b]
        first = True
        A[b + 1, 0:1, :, :] = jnp.zeros((1,) + A.shape[2:], F32)
        A[b + 1, rows + 1:rows + 2, :, :] = jnp.zeros((1,) + A.shape[2:], F32)
        if b == 0:
            A[b + 1, rows:rows + 1, :, :] = jnp.zeros((1,) + A.shape[2:], F32)
        for k in ks:
            a = DIRS[k][0]
            e = expert_of(k)
            ret = lax.dot_general(PG[e].reshape(rows * cols, ch), W[e],
                                  (((1,), (1,)), ((), ())), preferred_element_type=F32)
            ret = ret.reshape(rows, cols, ch)
            if first:
                A[b + 1, 1 + a:1 + a + rows, 8:8 + cols, :] = ret
                if b != 0:
                    A[b + 1, rows:rows + 1, 8:8 + cols, :] = jnp.zeros((1, cols, ch), F32)
                first = False
            else:
                A[b + 1, 1 + a:1 + a + rows, 8:8 + cols, :] += ret

    def colcopy(side_i, a):
        m = side_i * 3 + a + 1
        b = 2 * side_i - 1
        return rcopy(CS.at[side_i], CV.at[m], gs.at[m], gr.at[m],
                     lat + a, (lon + b + nlon) % nlon)

    def rowcopy(a):
        m = 6 + (a + 1) // 2
        return rcopy(RS.at[(a + 1) // 2], RV.at[(a + 1) // 2], gs.at[m], gr.at[m], lat + a, lon)

    back(-1)
    stage_x(nlat - 1)
    stage_z(nlat - 2)
    for r in range(rows + 2):
        CS[0, r:r + 1, :] = A[0, r, 8:9, :]
    CS[0, rows + 2:16, :] = jnp.zeros((14 - rows, ch), F32)
    for a in (-1, 0, 1):
        where_ok(lat + a, lambda a=a: colcopy(0, a).start())
    each(lambda j: tcopy(j).start())
    TR[me] = T[...]
    back(1)
    for r in range(rows + 2):
        CS[1, r:r + 1, :] = A[2, r, 7 + cols:8 + cols, :]
    CS[1, rows + 2:16, :] = jnp.zeros((14 - rows, ch), F32)
    for a in (-1, 0, 1):
        where_ok(lat + a, lambda a=a: colcopy(1, a).start())
    back(0)
    for h, r in ((0, 0), (1, rows + 1)):
        RS[h] = (A[1, r, 8:8 + cols] + A[0, r, 9:9 + cols] + A[2, r, 7:7 + cols]).astype(BF16)
    for a in (-1, 1):
        where_ok(lat + a, lambda a=a: rowcopy(a).start())

    xcopy(nlat - 1).wait_recv()
    total = KP[nlat - 1] + XR[nlat - 1].astype(F32)
    for s in range(nlat - 1):
        zcopy(s).wait_recv()
        total = total + ZR[s].astype(F32)
    G[...] = total
    sq = jnp.sum((total * total).reshape(ch // 16, 8, ch), axis=0)
    Q[...] = sq[:, :128] + sq[:, 128:]
    each(lambda j: qcopy(j).start())
    QR[me] = Q[...]

    for side_i in (0, 1):
        col = (8 + cols, 7)[side_i]
        acc = 2 * side_i
        colcopy(side_i, 0).wait_recv()
        for i in range(rows):
            A[acc, 1 + i, col:col + 1, :] = CV[side_i * 3 + 1, 1 + i:2 + i, :]

        def from_below(side_i=side_i, acc=acc, col=col):
            colcopy(side_i, -1).wait_recv()
            A[acc, rows, col:col + 1, :] += CV[side_i * 3, 0:1, :]

        def from_above(side_i=side_i, acc=acc, col=col):
            colcopy(side_i, 1).wait_recv()
            A[acc, 1, col:col + 1, :] += CV[side_i * 3 + 2, rows + 1:rows + 2, :]
        where_ok(lat + 1, from_below)
        where_ok(lat - 1, from_above)

    def row_below():
        rowcopy(-1).wait_recv()
        A[1, rows, 8:8 + cols, :] += RV[0].astype(F32)

    def row_above():
        rowcopy(1).wait_recv()
        A[1, 1, 8:8 + cols, :] += RV[1].astype(F32)
    where_ok(lat + 1, row_below)
    where_ok(lat - 1, row_above)
    for i in range(rows):
        GF[i] = (CT[i].astype(F32) + A[1, 1 + i, 8:8 + cols] + A[0, 1 + i, 9:9 + cols]
                 + A[2, 1 + i, 7:7 + cols]).astype(BF16)
    out = pltpu.make_async_copy(GF, gf, lsem.at[3])
    out.start()

    each(lambda j: tcopy(j).wait_recv())
    table = TR[0]
    for j in range(1, size):
        table = table + TR[j]
    each(lambda j: qcopy(j).wait_recv())
    sq = QR[0]
    for j in range(1, size):
        sq = sq + QR[j]
    squares = jnp.sum(sq, keepdims=True) + jnp.sum(table * table, keepdims=True)
    factor = jnp.minimum(1.0, 512.0 / jnp.sqrt(squares + 1e-06))
    gw[...] = G[...] * factor
    scaled = table * factor
    gt[...] = scaled[:, :gt.shape[1]]

    out.wait()
    for m, (a, b) in enumerate(DIRS):
        where_ok(lat + a, lambda m=m: halo(m).wait_send())
    for i in range(2 * nlat):
        ccopy(i).wait_send()
    for s in range(nlat):
        xcopy(s).wait_send()
    for s in range(nlat - 1):
        zcopy(s).wait_send()
    each(lambda j: tcopy(j).wait_send())
    each(lambda j: qcopy(j).wait_send())
    for side_i in (0, 1):
        for a in (-1, 0, 1):
            where_ok(lat + a, lambda side_i=side_i, a=a: colcopy(side_i, a).wait_send())
    for a in (-1, 1):
        where_ok(lat + a, lambda a=a: rowcopy(a).wait_send())


def place(a, b, c, x, y, z):
    x[...] = a[...]
    y[...] = b[...]
    z[...] = c[...]


def fused_body(features, cotangent, weights, coef_table, lat_index, dir_ids):
    nlat, nlon = lax.axis_size("lat"), lax.axis_size("lon")
    rows, cols, ch = features.shape
    experts = weights.shape[0]
    table_rows = coef_table.shape[0]
    lanes = -(-table_rows // 128) * 128
    size = nlat * nlon
    half = ch // 2
    V = pltpu.VMEM
    D = pltpu.SemaphoreType.DMA
    any_spec = pl.BlockSpec(memory_space=pl.ANY)
    smem = pl.BlockSpec(memory_space=pltpu.SMEM)
    vmem = pl.BlockSpec(memory_space=pltpu.VMEM)
    cells = rows * cols
    found = pl.pallas_call(
        functools.partial(fused, nlat, nlon),
        out_shape=(jax.ShapeDtypeStruct(features.shape, BF16),
                   jax.ShapeDtypeStruct((half, ch), F32),
                   jax.ShapeDtypeStruct((experts, table_rows), F32)),
        in_specs=[any_spec] * 3 + [smem] * 3,
        out_specs=(any_spec, vmem, vmem),
        scratch_shapes=[
            V((rows + 2, cols + 32, ch), BF16),
            V((rows, cols, ch), BF16),
            V((experts, ch, ch), BF16),
            V((rows + 2, cols + 32, ch), F32),
            V((3 * (rows + 2), cols, ch), BF16),
            V((experts, rows, cols, ch), BF16),
            V((experts, 2, half, ch), F32),
            V((experts, half, ch), F32),
            V((nlat, half, ch), BF16),
            V((nlat, half, ch), BF16),
            V((nlat, half, ch), F32),
            V((nlat - 1, half, ch), BF16),
            V((nlat - 1, half, ch), BF16),
            V((3, rows + 2, cols + 16, ch), F32),
            V((experts, lanes), F32),
            V((size, experts, lanes), F32),
            V((8, 128), F32),
            V((size, 8, 128), F32),
            V((rows, lanes), F32),
            V((2, 16, ch), F32),
            V((6, 16, ch), F32),
            V((2, cols, ch), BF16),
            V((2, cols, ch), BF16),
            V((half, ch), F32),
            V((rows, cols, ch), BF16),
            D((4,)), D((8,)), D((8,)), D((experts,)), D((experts,)),
            D((nlat,)), D((nlat,)), D((nlat,)), D((nlat,)),
            D((size,)), D((size,)), D((size,)), D((size,)), D((8,)), D((8,)),
        ],
        compiler_params=pltpu.CompilerParams(
            collective_id=0, has_side_effects=True, vmem_limit_bytes=62 * 1024 * 1024),
        cost_estimate=pl.CostEstimate(flops=6 * experts * cells * ch * ch,
                                      bytes_accessed=4 * 1024 * 1024,
                                      transcendentals=experts * cells * ch),
        name="relation_backward",
    )(features, cotangent, weights, coef_table.T, lat_index, dir_ids)
    grad_features, grad_weights, grad_table = pl.pallas_call(
        place,
        out_shape=[jax.ShapeDtypeStruct(x.shape, x.dtype) for x in found],
        in_specs=[vmem] * 3,
        out_specs=[vmem] * 3,
        compiler_params=pltpu.CompilerParams(vmem_limit_bytes=62 * 1024 * 1024),
        name="place_results",
    )(*found)
    return grad_features, grad_weights, grad_table.T


STEP_PAIRS = ((-1, -1), (-1, 0), (-1, 1), (0, -1), (0, 1), (1, -1), (1, 0), (1, 1))
clip_norm = 512.0


def with_halo(block, sides, width):
    for axis, dim in sides:
        count = lax.axis_size(axis)
        forward = [(i, i + 1) for i in range(count - 1)]
        forward.append((count - 1, 0))
        backward = [(target, source) for source, target in forward]
        low = lax.ppermute(
            lax.slice_in_dim(block, block.shape[dim] - width, None, axis=dim), axis, forward
        )
        high = lax.ppermute(lax.slice_in_dim(block, 0, width, axis=dim), axis, backward)
        block = jnp.concatenate([low, block, high], axis=dim)
    return block


def body(features, cotangent, weights, coef_table, lat_index, dir_ids):
    lat_rows, lon_cols, latent = features.shape
    experts = weights.shape[0]
    global_rows = coef_table.shape[0]
    lat_size = lax.axis_size("lat")
    lat_pos = lax.axis_index("lat")
    keep_top = (lat_pos > 0).astype(jnp.float32)
    keep_bottom = (lat_pos < lat_size - 1).astype(jnp.float32)
    padded = with_halo(features, (("lat", 0), ("lon", 1)), 1)
    padded = jnp.concatenate(
        [
            padded[:1] * keep_top.astype(jnp.bfloat16),
            padded[1:-1],
            padded[-1:] * keep_bottom.astype(jnp.bfloat16),
        ],
        axis=0,
    )
    shifted = jnp.stack(
        [
            padded[1 + lat_step : 1 + lat_step + lat_rows, 1 + lon_step : 1 + lon_step + lon_cols]
            for lat_step, lon_step in STEP_PAIRS
        ]
    )
    neighbours = jnp.take(shifted, dir_ids, axis=0).reshape(experts, lat_rows * lon_cols, latent)
    preact = jnp.einsum("epc,ecd->epd", neighbours, weights, preferred_element_type=jnp.float32)
    logistic = jax.nn.sigmoid(preact)
    activated = (preact * logistic).reshape(experts, lat_rows, lon_cols, latent)
    derivative = (logistic * (1.0 + preact * (1.0 - logistic))).reshape(
        experts, lat_rows, lon_cols, latent
    )
    picker = (lat_index[:, None] == jnp.arange(global_rows, dtype=jnp.int32)[None, :]).astype(
        jnp.float32
    )
    row_coef = jnp.dot(picker, coef_table, precision=lax.Precision.HIGHEST)
    grad32 = cotangent.astype(jnp.float32)
    row_sums = jnp.sum(grad32[None] * activated, axis=(2, 3))
    table_part = jnp.dot(picker.T, row_sums.T, precision=lax.Precision.HIGHEST)
    pre_grad = (grad32[None] * row_coef.T[:, :, None, None] * derivative).astype(jnp.bfloat16)
    pre_grad = pre_grad.reshape(experts, lat_rows * lon_cols, latent)
    weight_part = jnp.einsum(
        "epc,epd->ecd", neighbours, pre_grad, preferred_element_type=jnp.float32
    ).reshape(experts * latent, latent)
    returned = jnp.einsum(
        "epd,ecd->epc", pre_grad, weights, preferred_element_type=jnp.float32
    ).reshape(experts, lat_rows, lon_cols, latent)
    inverse = jnp.argsort(dir_ids)
    by_direction = jnp.take(returned, inverse, axis=0)
    spread = jnp.zeros((lat_rows + 2, lon_cols + 2, latent), jnp.float32)
    for index, (lat_step, lon_step) in enumerate(STEP_PAIRS):
        spread = spread + jnp.pad(
            by_direction[index],
            ((1 + lat_step, 1 - lat_step), (1 + lon_step, 1 - lon_step), (0, 0)),
        )
    rimmed = with_halo(spread, (("lat", 0), ("lon", 1)), 1)
    folded = rimmed[:, 2 : lon_cols + 2]
    folded = folded.at[:, 0].add(rimmed[:, 0]).at[:, lon_cols - 1].add(rimmed[:, lon_cols + 3])
    interior = folded[2 : lat_rows + 2]
    interior = (
        interior.at[0]
        .add(folded[0] * keep_top)
        .at[lat_rows - 1]
        .add(folded[lat_rows + 3] * keep_bottom)
    )
    grad_features = (grad32 + interior).astype(jnp.bfloat16)
    table_grad = lax.psum(table_part, ("lat", "lon"))
    weight_shard = lax.psum_scatter(weight_part, ("lat", "lon"), scatter_dimension=0, tiled=True)
    shard_squares = lax.psum(jnp.sum(weight_shard * weight_shard), ("lat", "lon"))
    squares = shard_squares + jnp.sum(table_grad * table_grad)
    factor = jnp.minimum(1.0, clip_norm / jnp.sqrt(squares + 1e-06))
    return (grad_features, factor * weight_shard, factor * table_grad)


def solution(mesh):
    in_specs = (
        P(("grp", "lat"), "lon", None),
        P(("grp", "lat"), "lon", None),
        P(),
        P(),
        P("lat"),
        P(),
    )
    out_specs = (P(("grp", "lat"), "lon", None), P(("grp", "lat", "lon"), None), P("grp", None))
    fits = mesh.shape["lat"] == 4 and mesh.shape["lon"] == 4
    chosen = fused_body if fits else body
    return jax.shard_map(chosen, mesh=mesh, in_specs=in_specs, out_specs=out_specs, check_vma=False)
```
